32 devices in a mesh: blocks: 8 (over y, x, core), phi: 4 (over z).
Axes of the slice: x: 2, y: 2, z: 4, core: 2. Of those that a mesh axis runs over, the one named last changes fastest.
Arguments:
- field: float32 [3, 128, 64, 512], P(None, 'blocks', 'phi'), may hold values from -6 to 6
- velocity: float32 [3, 128, 64, 512], P(None, 'blocks', 'phi'), may hold values from -6 to 6
- strip_shift: int32 [128], P('blocks'), may hold values from 0 to 6, as said below
- strip_frac: float32 [128], P('blocks'), may hold values from 0 to 1
- edge_shift: int32 [2], replicated, may hold values from 0 to 6, as said below
- edge_frac: float32 [2], replicated, may hold values from 0 to 1
Outputs:
- advected: float32 [3, 128, 64, 512], P(None, 'blocks', 'phi')
The draws below stay inside these ranges and needn't reach their ends.
Inputs may be any that keep to these rules, and one draw needn't show every extreme that they name: `strip_shift`: some strip has a shift of exactly 6 and some strip a shift of 0. `edge_shift`: exactly one of the two boundary offsets equals 6; the other is smaller.
All inputs are finite; a program needn't handle non-finite values.
Results may differ from the reference program's by a relative error of at most 0.00002.
Values sent between devices are 32-bit elements; how exact they have to be, the bound alone decides.
A program may use at most 128 MiB of HBM per device.

```python
import jax
import jax.numpy as jnp

NZ = 512
KMAX = 6
NX = 128
NY = 64


def draw_strip_shift(key, part):
    source_key, spot_key = jax.random.split(jax.random.fold_in(key, 11))
    values = jax.random.randint(source_key, (NX,), 0, KMAX + 1, dtype=jnp.int32)
    spot = jax.random.randint(spot_key, (), 0, NX, dtype=jnp.int32)
    other = (spot + 1) % NX
    places = jnp.arange(NX, dtype=jnp.int32)
    values = jnp.where(places == other, 0, values)
    return jnp.where(places == spot, KMAX, values).astype(jnp.int32)


def draw_edge_shift(key, part):
    source_key, spot_key = jax.random.split(jax.random.fold_in(key, 23))
    values = jax.random.randint(source_key, (2,), 0, KMAX, dtype=jnp.int32)
    spot = jax.random.randint(spot_key, (), 0, 2, dtype=jnp.int32)
    return jnp.where(jnp.arange(2, dtype=jnp.int32) == spot, KMAX, values).astype(jnp.int32)


def block_scale(own_key, shape, pieces, smallest, top_value):
    def one(position, blocks):
        heights = jax.random.uniform(jax.random.fold_in(jax.random.fold_in(own_key, 6), position), (blocks,), jnp.float32, smallest / len(pieces), top_value / len(pieces))
        return jnp.repeat(jnp.exp(heights), shape[position] // blocks).reshape((-1,) + (1,) * (len(shape) - position - 1))

    factor_of = one(*pieces[0])
    for cut in pieces[1:]:
        factor_of = factor_of * one(*cut)
    return factor_of


def centred(stream_key, shape, width, bound, shards=(), kind=jnp.bfloat16):
    factor_of = block_scale(stream_key, shape, shards, -0.22, 0.18) if shards else 1.0
    drawn = jax.random.normal(stream_key, shape, jnp.float32) * width * factor_of
    return jnp.minimum(jnp.maximum(drawn, -bound), bound).astype(kind)


def setup_inputs(seed: int = 0) -> dict:
    streams_of = jax.random.split(jax.random.key(seed), 7)
    return {
        "field": centred(streams_of[0], (3, NX, NY, NZ), 1.0, 6.0, ((1, 8), (2, 4)), jnp.float32),
        "velocity": centred(streams_of[1], (3, NX, NY, NZ), 1.0, 6.0, ((1, 8), (2, 4)), jnp.float32),
        "strip_shift": draw_strip_shift(jax.random.fold_in(streams_of[6], 71), 0),
        "strip_frac": jnp.clip(1.0 * jax.random.uniform(streams_of[3], (NX,), jnp.float32) ** block_scale(streams_of[3], (NX,), ((0, 8),), -0.2, 0.2), 0.0, 1.0),
        "edge_shift": draw_edge_shift(jax.random.fold_in(streams_of[6], 71), 0),
        "edge_frac": jnp.clip(jax.random.uniform(streams_of[5], (2,), jnp.float32, 0.0, 1.0), 0.0, 1.0),
    }


COURANT = 0.4


def below(values):
    return jnp.roll(values, 1, axis=-1)


def above(values):
    return jnp.roll(values, -1, axis=-1)


def ct_update(padded):
    field_x, field_y, field_z = padded[0], padded[1], padded[2]
    flow_x, flow_y, flow_z = padded[3], padded[4], padded[5]
    zedge_fx = 0.5 * (field_x[1:, 1:] + field_x[1:, :-1])
    zedge_fy = 0.5 * (field_y[1:, 1:] + field_y[:-1, 1:])
    zedge_vx = 0.25 * (flow_x[1:, 1:] + flow_x[:-1, 1:] + flow_x[1:, :-1] + flow_x[:-1, :-1])
    zedge_vy = 0.25 * (flow_y[1:, 1:] + flow_y[:-1, 1:] + flow_y[1:, :-1] + flow_y[:-1, :-1])
    emf_z = zedge_vy * zedge_fx - zedge_vx * zedge_fy
    middle_fx = field_x[:, 1:-1]
    middle_fz = field_z[:, 1:-1]
    middle_vx = flow_x[:, 1:-1]
    middle_vz = flow_z[:, 1:-1]
    yedge_fx = 0.5 * (middle_fx[1:] + below(middle_fx[1:]))
    yedge_fz = 0.5 * (middle_fz[1:] + middle_fz[:-1])
    paired_vx = middle_vx[1:] + middle_vx[:-1]
    paired_vz = middle_vz[1:] + middle_vz[:-1]
    yedge_vx = 0.25 * (paired_vx + below(paired_vx))
    yedge_vz = 0.25 * (paired_vz + below(paired_vz))
    emf_y = yedge_vx * yedge_fz - yedge_vz * yedge_fx
    radial_fy = field_y[1:-1]
    radial_fz = field_z[1:-1]
    radial_vy = flow_y[1:-1]
    radial_vz = flow_z[1:-1]
    xedge_fy = 0.5 * (radial_fy[:, 1:] + below(radial_fy[:, 1:]))
    xedge_fz = 0.5 * (radial_fz[:, 1:] + radial_fz[:, :-1])
    couple_vy = radial_vy[:, 1:] + radial_vy[:, :-1]
    couple_vz = radial_vz[:, 1:] + radial_vz[:, :-1]
    xedge_vy = 0.25 * (couple_vy + below(couple_vy))
    xedge_vz = 0.25 * (couple_vz + below(couple_vz))
    emf_x = xedge_vz * xedge_fy - xedge_vy * xedge_fz
    radial_count = emf_x.shape[0]
    azimuth_count = emf_y.shape[1]
    new_x = field_x[1:-1, 1:-1] - COURANT * ((emf_z[:radial_count, 1:] - emf_z[:radial_count, :azimuth_count]) - (above(emf_y[:radial_count]) - emf_y[:radial_count]))
    new_y = field_y[1:-1, 1:-1] - COURANT * ((above(emf_x[:, :azimuth_count]) - emf_x[:, :azimuth_count]) - (emf_z[1:, :azimuth_count] - emf_z[:radial_count, :azimuth_count]))
    new_z = field_z[1:-1, 1:-1] - COURANT * ((emf_y[1:] - emf_y[:radial_count]) - (emf_x[:, 1:] - emf_x[:, :azimuth_count]))
    return jnp.stack([new_x, new_y, new_z])


def lower_remap(rows, shift, weight):
    return (1.0 - weight) * jnp.roll(rows, shift, axis=1) + weight * jnp.roll(rows, shift + 1, axis=1)


def upper_remap(rows, shift, weight):
    return (1.0 - weight) * jnp.roll(rows, -shift, axis=1) + weight * jnp.roll(rows, -shift - 1, axis=1)


def reference(field, velocity, strip_shift, strip_frac, edge_shift, edge_frac):
    stacked = jnp.concatenate([field, velocity], axis=0)
    inner_ghost = lower_remap(stacked[:, -1], edge_shift[0], edge_frac[0])
    outer_ghost = upper_remap(stacked[:, 0], edge_shift[1], edge_frac[1])
    widened = jnp.concatenate([inner_ghost[:, None], stacked, outer_ghost[:, None]], axis=1)
    padded = jnp.concatenate([widened[:, :, -1:], widened, widened[:, :, :1]], axis=2)
    updated = ct_update(padded)

    def one_strip(rows, shift, weight):
        return lower_remap(rows, shift, weight)

    return jax.vmap(one_strip, in_axes=(1, 0, 0), out_axes=1)(updated, strip_shift, strip_frac)
```

```python
import functools

import jax
import jax.numpy as jnp
from jax import lax
from jax.experimental import pallas as pl
from jax.experimental.pallas import tpu as pltpu
from jax.sharding import PartitionSpec as P

COURANT = 0.4
SCALE = COURANT * 0.125
MESH = pl.DeviceIdType.MESH


def kernel(
    blocks,
    phis,
    field,
    velocity,
    strip_shift,
    strip_frac,
    edge_shift,
    edge_frac,
    out,
    ext,
    low_raw,
    high_raw,
    low_corner,
    high_corner,
    row_send,
    row_recv,
    top_edges,
    bottom_edges,
    edge_send,
    edge_recv,
    updated,
    pack_a,
    pack_b,
    near_a,
    near_b,
    result,
    load_sem,
    store_sem,
    send_sem,
    recv_sem,
):
    b = lax.axis_index("blocks")
    p = lax.axis_index("phi")
    b_up = lax.rem(b + 1, blocks)
    b_down = lax.rem(b + blocks - 1, blocks)
    p_up = lax.rem(p + 1, phis)
    p_down = lax.rem(p + phis - 1, phis)
    first = b == 0
    last = b == blocks - 1
    strips = field.shape[1]
    wide = field.shape[3]

    loads = [
        pltpu.make_async_copy(
            source.at[:, :, rows, :],
            ext.at[part, 1 : strips + 1, pl.ds(8 + rows.start, 8), :],
            load_sem.at[n],
        )
        for n, (source, part, rows) in enumerate(
            (
                (field, slice(0, 3), slice(8, 16)),
                (velocity, slice(3, 6), slice(8, 16)),
                (field, slice(0, 3), slice(0, 8)),
                (velocity, slice(3, 6), slice(0, 8)),
            )
        )
    ]
    for load in loads:
        load.start()

    barrier = pltpu.get_barrier_semaphore()
    for device in ((b_up, p), (b_down, p), (b, p_up), (b, p_down)):
        pl.semaphore_signal(barrier, inc=1, device_id=device, device_id_type=MESH)

    @pl.when(first)
    def _():
        pl.semaphore_signal(barrier, inc=1, device_id=(b_down, p_down), device_id_type=MESH)

    @pl.when(last)
    def _():
        pl.semaphore_signal(barrier, inc=1, device_id=(b_up, p_up), device_id_type=MESH)

    pl.semaphore_wait(barrier, jnp.where(jnp.logical_or(first, last), 5, 4))

    def remote(n, source, target, device):
        return pltpu.make_async_remote_copy(
            src_ref=source,
            dst_ref=target,
            send_sem=send_sem.at[n],
            recv_sem=recv_sem.at[n],
            device_id=device,
            device_id_type=MESH,
        )

    end = strips - 1
    up_f = remote(0, field.at[1:3, end], low_raw.at[1:3, 8:24], (b_up, p))
    up_v = remote(1, velocity.at[:, end], low_raw.at[3:6, 8:24], (b_up, p))
    down_f = remote(2, field.at[:, 0], high_raw.at[0:3, 8:24], (b_down, p))
    down_v = remote(3, velocity.at[:, 0], high_raw.at[3:6, 8:24], (b_down, p))
    shear_up_f = remote(4, field.at[1:3, end, 8:16], low_raw.at[1:3, 0:8], (b_up, p_up))
    shear_up_v = remote(5, velocity.at[:, end, 8:16], low_raw.at[3:6, 0:8], (b_up, p_up))
    shear_down_f = remote(6, field.at[:, 0, 0:8], high_raw.at[0:3, 24:32], (b_down, p_down))
    shear_down_v = remote(7, velocity.at[:, 0, 0:8], high_raw.at[3:6, 24:32], (b_down, p_down))
    row_up = remote(8, row_send, row_recv, (b, p_up))
    corner_up = remote(9, row_recv.at[1:3, strips - 8 : strips], low_corner, (b_up, p))
    corner_down = remote(10, row_recv.at[0:3, 0:8], high_corner, (b_down, p))
    near_copy_a = remote(11, pack_a, near_a.at[:, 0:7, 0:8], (b, p_up))
    near_copy_b = remote(12, pack_b, near_b.at[:, 0:7, 0:8], (b, p_up))
    edges_down = remote(13, edge_send, edge_recv, (b, p_down))

    for copy in (up_f, up_v, down_f, down_v):
        copy.start()

    @pl.when(last)
    def _():
        shear_up_f.start()
        shear_up_v.start()

    @pl.when(first)
    def _():
        shear_down_f.start()
        shear_down_v.start()

    row_parts = (0, 3, 4, 5, 2)
    loads[0].wait()
    loads[1].wait()
    for n, part in enumerate(row_parts):
        for i in range(strips):
            row_send[n, i : i + 1, :] = ext[part, i + 1, 23:24, :]
    row_up.start()
    loads[2].wait()
    loads[3].wait()

    level = lax.broadcasted_iota(jnp.int32, (8, wide), 0)

    def below(values):
        return pltpu.roll(values, 1, axis=1)

    def above(values):
        return pltpu.roll(values, wide - 1, axis=1)

    def side_edges(i, row):
        here = lambda part: ext[part, i + 1, row : row + 8, :]
        inner = lambda part: ext[part, i, row : row + 8, :]
        here_low = lambda part: ext[part, i + 1, row - 1 : row + 7, :]
        inner_low = lambda part: ext[part, i, row - 1 : row + 7, :]
        fx = here(0)
        vx = here(3) + inner(3)
        vz = here(5) + inner(5)
        vx_all = vx + here_low(3) + inner_low(3)
        vy_all = here(4) + inner(4) + here_low(4) + inner_low(4)
        emf_z = vy_all * (fx + here_low(0)) - vx_all * (here(1) + inner(1))
        emf_y = (vx + below(vx)) * (here(2) + inner(2)) - (vz + below(vz)) * (fx + below(fx))
        return emf_z, emf_y

    def cross_edge(i, row):
        here = lambda part: ext[part, i + 1, row : row + 8, :]
        here_low = lambda part: ext[part, i + 1, row - 1 : row + 7, :]
        fy = here(1)
        vy = here(4) + here_low(4)
        vz = here(5) + here_low(5)
        return (vz + below(vz)) * (fy + below(fy)) - (vy + below(vy)) * (here(2) + here_low(2))

    def new_cells(i, row, emf_z, emf_y, emf_x, next_z, next_y, beyond_z, beyond_x):
        lift = lambda values, beyond: jnp.where(level == 7, beyond, pltpu.roll(values, 7, axis=0))
        new_x = ext[0, i + 1, row : row + 8, :] - SCALE * (
            (lift(emf_z, beyond_z) - emf_z) - (above(emf_y) - emf_y)
        )
        new_y = ext[1, i + 1, row : row + 8, :] - SCALE * (
            (above(emf_x) - emf_x) - (next_z - emf_z)
        )
        new_z = ext[2, i + 1, row : row + 8, :] - SCALE * (
            (next_y - emf_y) - (lift(emf_x, beyond_x) - emf_x)
        )
        return new_x, new_y, new_z

    def upper_rows(start, count, pack, offset):
        def step(n, carried):
            i = start + n
            emf_z, emf_y = carried
            next_z, next_y = side_edges(i + 1, 16)
            emf_x = cross_edge(i, 16)
            top_edges[0, i] = emf_z
            top_edges[1, i] = emf_x
            cells = new_cells(i, 16, emf_z, emf_y, emf_x, next_z, next_y, 0.0, 0.0)
            for part, values in enumerate(cells):
                updated[part, i, 8:16, :] = values
                pack[part, n + offset] = values
            return next_z, next_y

        lax.fori_loop(0, count, step, side_edges(start, 16))

    def spread_last(pack, strip):
        for part in range(3):
            for n in range(7):
                pack[part, n, 0:1, :] = updated[part, strip, 9 + n : 10 + n, :]

    quarter = strips // 4
    half = strips // 2
    upper_rows(quarter, half - 1, pack_a, 0)

    def one_upper(i):
        emf_z, emf_y = side_edges(i, 16)
        next_z, next_y = side_edges(i + 1, 16)
        emf_x = cross_edge(i, 16)
        top_edges[0, i] = emf_z
        top_edges[1, i] = emf_x
        cells = new_cells(i, 16, emf_z, emf_y, emf_x, next_z, next_y, 0.0, 0.0)
        for part, values in enumerate(cells):
            updated[part, i, 8:16, :] = values

    one_upper(quarter + half - 1)
    spread_last(pack_a, quarter + half - 1)
    near_copy_a.start()

    for copy in (up_f, up_v, down_f, down_v):
        copy.wait_recv()

    @pl.when(first)
    def _():
        shear_up_f.wait_recv()
        shear_up_v.wait_recv()
        shift = edge_shift[0]
        weight = edge_frac[0]
        for part in range(1, 6):
            rows = low_raw[part]
            mixed = (1.0 - weight) * rows + weight * pltpu.roll(rows, 1, axis=0)
            ext[part, 0, :, :] = pltpu.roll(mixed, shift, axis=0)

    @pl.when(jnp.logical_not(first))
    def _():
        for part in range(1, 6):
            ext[part, 0, 8:24, :] = low_raw[part, 8:24, :]

    @pl.when(last)
    def _():
        shear_down_f.wait_recv()
        shear_down_v.wait_recv()
        shift = edge_shift[1]
        weight = edge_frac[1]
        for part in range(6):
            rows = high_raw[part]
            mixed = (1.0 - weight) * rows + weight * pltpu.roll(rows, 31, axis=0)
            ext[part, strips + 1, 8:24, :] = pltpu.roll(mixed, lax.rem(32 - shift, 32), axis=0)[8:24]

    @pl.when(jnp.logical_not(last))
    def _():
        for part in range(6):
            ext[part, strips + 1, 8:24, :] = high_raw[part, 8:24, :]

    row_up.wait_recv()
    corner_up.start()
    corner_down.start()

    upper_rows(strips - quarter, quarter, pack_b, 0)
    upper_rows(0, quarter - 1, pack_b, quarter)
    one_upper(quarter - 1)
    spread_last(pack_b, quarter - 1)
    near_copy_b.start()

    for n, part in enumerate(row_parts):
        for i in range(strips):
            ext[part, i + 1, 7:8, :] = row_recv[n, i : i + 1, :]

    corner_up.wait_recv()
    corner_down.wait_recv()

    @pl.when(jnp.logical_not(first))
    def _():
        for n, part in enumerate((3, 4)):
            ext[part, 0, 7:8, :] = low_corner[n, 7:8, :]

    @pl.when(last)
    def _():
        shift = edge_shift[1]
        weight = edge_frac[1]
        for n, part in enumerate((0, 3, 4)):
            high_raw[part, 7:8, :] = high_corner[n, 0:1, :]
            rows = high_raw[part, 0:16, :]
            mixed = (1.0 - weight) * rows + weight * pltpu.roll(rows, 15, axis=0)
            ext[part, strips + 1, 7:8, :] = pltpu.roll(mixed, lax.rem(16 - shift, 16), axis=0)[7:8]

    @pl.when(jnp.logical_not(last))
    def _():
        for n, part in enumerate((0, 3, 4)):
            ext[part, strips + 1, 7:8, :] = high_corner[n, 0:1, :]

    def lower_rows(start, count, near, offset):
        def step(n, carried):
            i = start + n
            emf_z, emf_y = carried
            next_z, next_y = side_edges(i + 1, 8)
            emf_x = cross_edge(i, 8)
            bottom_edges[0, i] = emf_z
            bottom_edges[1, i] = emf_x
            cells = new_cells(
                i,
                8,
                emf_z,
                emf_y,
                emf_x,
                next_z,
                next_y,
                pltpu.roll(top_edges[0, i], 7, axis=0),
                pltpu.roll(top_edges[1, i], 7, axis=0),
            )
            for part, values in enumerate(cells):
                updated[part, i, 0:8, :] = values
                near[part, n + offset, 8:16, :] = values
            return next_z, next_y

        lax.fori_loop(0, count, step, side_edges(start, 8))

    lower_rows(0, quarter, near_b, quarter)
    lower_rows(quarter, half, near_a, 0)
    lower_rows(strips - quarter, quarter, near_b, 0)
    for n in range(2):
        for i in range(strips):
            edge_send[n, i : i + 1, :] = bottom_edges[n, i, 0:1, :]
    edges_down.start()

    edges_down.wait_recv()

    def blend_upper(i, _):
        updated[0, i, 15:16, :] = updated[0, i, 15:16, :] - SCALE * edge_recv[0, pl.ds(i, 1), :]
        updated[2, i, 15:16, :] = updated[2, i, 15:16, :] + SCALE * edge_recv[1, pl.ds(i, 1), :]
        shift = strip_shift[i]
        weight = strip_frac[i]
        for part in range(3):
            rows = updated[part, i]
            mixed = (1.0 - weight) * rows + weight * pltpu.roll(rows, 1, axis=0)
            result[part, i, 8:16, :] = pltpu.roll(mixed, shift, axis=0)[8:16]
        return 0

    lax.fori_loop(0, strips, blend_upper, 0)
    stores = [
        pltpu.make_async_copy(
            result.at[:, places, rows, :], out.at[:, places, rows, :], store_sem.at[n]
        )
        for n, (places, rows) in enumerate(
            (
                (slice(0, strips), slice(8, 16)),
                (slice(quarter, quarter + half), slice(0, 8)),
                (slice(strips - quarter, strips), slice(0, 8)),
                (slice(0, quarter), slice(0, 8)),
            )
        )
    ]
    stores[0].start()

    def blend_lower(near, start):
        for part in range(3):
            for n in range(7):
                near[part, 7, n + 1 : n + 2, :] = near[part, n, 0:1, :]

        def step(n, _):
            i = lax.rem(start + n, strips)
            near[0, n, 7:8, :] = near[0, n, 7:8, :] - SCALE * bottom_edges[0, i, 0:1, :]
            near[2, n, 7:8, :] = near[2, n, 7:8, :] + SCALE * bottom_edges[1, i, 0:1, :]
            shift = strip_shift[i]
            weight = strip_frac[i]
            for part in range(3):
                rows = near[part, n]
                mixed = (1.0 - weight) * rows + weight * pltpu.roll(rows, 1, axis=0)
                result[part, i, 0:8, :] = pltpu.roll(mixed, shift, axis=0)[8:16]
            return 0

        lax.fori_loop(0, half, step, 0)

    near_copy_a.wait_recv()
    blend_lower(near_a, quarter)
    stores[1].start()
    near_copy_b.wait_recv()
    blend_lower(near_b, strips - quarter)
    stores[2].start()
    stores[3].start()

    for copy in (up_f, up_v, down_f, down_v, row_up, corner_up, corner_down):
        copy.wait_send()
    for copy in (near_copy_a, near_copy_b, edges_down):
        copy.wait_send()

    @pl.when(last)
    def _():
        shear_up_f.wait_send()
        shear_up_v.wait_send()

    @pl.when(first)
    def _():
        shear_down_f.wait_send()
        shear_down_v.wait_send()

    for store in stores:
        store.wait()


def body(mesh_shape, field, velocity, strip_shift, strip_frac, edge_shift, edge_frac):
    parts, strips, azimuth, wide = field.shape
    half = strips // 2
    f32 = jnp.float32
    smem = pl.BlockSpec(memory_space=pltpu.SMEM)
    hbm = pl.BlockSpec(memory_space=pl.ANY)
    return pl.pallas_call(
        functools.partial(kernel, mesh_shape["blocks"], mesh_shape["phi"]),
        out_shape=jax.ShapeDtypeStruct(field.shape, f32),
        in_specs=[hbm, hbm, smem, smem, smem, smem],
        out_specs=hbm,
        scratch_shapes=[
            pltpu.VMEM((6, strips + 2, 8 + azimuth, wide), f32),
            pltpu.VMEM((6, 24, wide), f32),
            pltpu.VMEM((6, 32, wide), f32),
            pltpu.VMEM((2, 8, wide), f32),
            pltpu.VMEM((3, 8, wide), f32),
            pltpu.VMEM((5, strips, wide), f32),
            pltpu.VMEM((5, strips, wide), f32),
            pltpu.VMEM((2, strips, 8, wide), f32),
            pltpu.VMEM((2, strips, 8, wide), f32),
            pltpu.VMEM((2, strips, wide), f32),
            pltpu.VMEM((2, strips, wide), f32),
            pltpu.VMEM((3, strips, azimuth, wide), f32),
            pltpu.VMEM((3, 7, 8, wide), f32),
            pltpu.VMEM((3, 7, 8, wide), f32),
            pltpu.VMEM((3, half, 16, wide), f32),
            pltpu.VMEM((3, half, 16, wide), f32),
            pltpu.VMEM((3, strips, azimuth, wide), f32),
            pltpu.SemaphoreType.DMA((4,)),
            pltpu.SemaphoreType.DMA((4,)),
            pltpu.SemaphoreType.DMA((14,)),
            pltpu.SemaphoreType.DMA((14,)),
        ],
        compiler_params=pltpu.CompilerParams(
            collective_id=0, has_side_effects=True, vmem_limit_bytes=40 * 1024 * 1024
        ),
    )(field, velocity, strip_shift, strip_frac, edge_shift, edge_frac)


def solution(mesh):
    placed = (
        P(None, "blocks", "phi", None),
        P(None, "blocks", "phi", None),
        P("blocks"),
        P("blocks"),
        P(),
        P(),
    )
    return jax.shard_map(
        functools.partial(body, dict(mesh.shape)),
        mesh=mesh,
        in_specs=placed,
        out_specs=P(None, "blocks", "phi", None),
        check_vma=False,
    )
```

```python
import functools

import jax
import jax.numpy as jnp
from jax import lax
from jax.experimental import pallas as pl
from jax.experimental.pallas import tpu as pltpu
from jax.sharding import PartitionSpec as P

COURANT = 0.4
SCALE = COURANT * 0.125
MESH = pl.DeviceIdType.MESH


def kernel(
    blocks,
    phis,
    field,
    velocity,
    shift_in,
    frac_in,
    edge_shift_in,
    edge_frac_in,
    out,
    ext,
    low_raw,
    high_raw,
    low_corner,
    high_corner,
    row_send,
    row_recv,
    top_edges,
    bottom_edges,
    edge_send,
    edge_recv,
    updated,
    pack_a,
    pack_b,
    near_a,
    near_b,
    result,
    strip_shift,
    strip_frac,
    edge_shift,
    edge_frac,
    load_sem,
    store_sem,
    send_sem,
    recv_sem,
):
    b = lax.axis_index("blocks")
    p = lax.axis_index("phi")
    b_up = lax.rem(b + 1, blocks)
    b_down = lax.rem(b + blocks - 1, blocks)
    p_up = lax.rem(p + 1, phis)
    p_down = lax.rem(p + phis - 1, phis)
    first = b == 0
    last = b == blocks - 1
    strips = field.shape[1]
    wide = field.shape[3]

    loads = [
        pltpu.make_async_copy(
            source.at[:, :, rows, :],
            ext.at[part, 1 : strips + 1, pl.ds(8 + rows.start, 8), :],
            load_sem.at[n],
        )
        for n, (source, part, rows) in enumerate(
            (
                (field, slice(0, 3), slice(8, 16)),
                (velocity, slice(3, 6), slice(8, 16)),
                (field, slice(0, 3), slice(0, 8)),
                (velocity, slice(3, 6), slice(0, 8)),
            )
        )
    ]
    for load in loads:
        load.start()
    scalars = [
        pltpu.make_async_copy(source, target, load_sem.at[4 + n])
        for n, (source, target) in enumerate(
            (
                (shift_in, strip_shift),
                (frac_in, strip_frac),
                (edge_shift_in, edge_shift),
                (edge_frac_in, edge_frac),
            )
        )
    ]
    for copy in scalars:
        copy.start()

    barrier = pltpu.get_barrier_semaphore()
    for device in ((b_up, p), (b_down, p), (b, p_up), (b, p_down)):
        pl.semaphore_signal(barrier, inc=1, device_id=device, device_id_type=MESH)

    @pl.when(first)
    def _():
        pl.semaphore_signal(barrier, inc=1, device_id=(b_down, p_down), device_id_type=MESH)

    @pl.when(last)
    def _():
        pl.semaphore_signal(barrier, inc=1, device_id=(b_up, p_up), device_id_type=MESH)

    pl.semaphore_wait(barrier, jnp.where(jnp.logical_or(first, last), 5, 4))

    def remote(n, source, target, device):
        return pltpu.make_async_remote_copy(
            src_ref=source,
            dst_ref=target,
            send_sem=send_sem.at[n],
            recv_sem=recv_sem.at[n],
            device_id=device,
            device_id_type=MESH,
        )

    end = strips - 1
    up_f = remote(0, field.at[1:3, end], low_raw.at[1:3, 8:24], (b_up, p))
    up_v = remote(1, velocity.at[:, end], low_raw.at[3:6, 8:24], (b_up, p))
    down_f = remote(2, field.at[:, 0], high_raw.at[0:3, 8:24], (b_down, p))
    down_v = remote(3, velocity.at[:, 0], high_raw.at[3:6, 8:24], (b_down, p))
    shear_up_f = remote(4, field.at[1:3, end, 8:16], low_raw.at[1:3, 0:8], (b_up, p_up))
    shear_up_v = remote(5, velocity.at[:, end, 8:16], low_raw.at[3:6, 0:8], (b_up, p_up))
    shear_down_f = remote(6, field.at[:, 0, 0:8], high_raw.at[0:3, 24:32], (b_down, p_down))
    shear_down_v = remote(7, velocity.at[:, 0, 0:8], high_raw.at[3:6, 24:32], (b_down, p_down))
    row_up = remote(8, row_send, row_recv, (b, p_up))
    corner_up = remote(9, row_recv.at[1:3, strips - 8 : strips], low_corner, (b_up, p))
    corner_down = remote(10, row_recv.at[0:3, 0:8], high_corner, (b_down, p))
    near_copy_a = remote(11, pack_a, near_a.at[:, 0:7, 0:8], (b, p_up))
    near_copy_b = remote(12, pack_b, near_b.at[:, 0:7, 0:8], (b, p_up))
    edges_down = remote(13, edge_send, edge_recv, (b, p_down))

    for copy in (up_f, up_v, down_f, down_v):
        copy.start()

    @pl.when(last)
    def _():
        shear_up_f.start()
        shear_up_v.start()

    @pl.when(first)
    def _():
        shear_down_f.start()
        shear_down_v.start()

    row_parts = (0, 3, 4, 5, 2)
    loads[0].wait()
    loads[1].wait()
    for n, part in enumerate(row_parts):
        for i in range(strips):
            row_send[n, i : i + 1, :] = ext[part, i + 1, 23:24, :]
    row_up.start()
    loads[2].wait()
    loads[3].wait()

    level = lax.broadcasted_iota(jnp.int32, (8, wide), 0)

    def below(values):
        return pltpu.roll(values, 1, axis=1)

    def above(values):
        return pltpu.roll(values, wide - 1, axis=1)

    def side_edges(i, row):
        here = lambda part: ext[part, i + 1, row : row + 8, :]
        inner = lambda part: ext[part, i, row : row + 8, :]
        here_low = lambda part: ext[part, i + 1, row - 1 : row + 7, :]
        inner_low = lambda part: ext[part, i, row - 1 : row + 7, :]
        fx = here(0)
        vx = here(3) + inner(3)
        vz = here(5) + inner(5)
        vx_all = vx + here_low(3) + inner_low(3)
        vy_all = here(4) + inner(4) + here_low(4) + inner_low(4)
        emf_z = vy_all * (fx + here_low(0)) - vx_all * (here(1) + inner(1))
        emf_y = (vx + below(vx)) * (here(2) + inner(2)) - (vz + below(vz)) * (fx + below(fx))
        return emf_z, emf_y

    def cross_edge(i, row):
        here = lambda part: ext[part, i + 1, row : row + 8, :]
        here_low = lambda part: ext[part, i + 1, row - 1 : row + 7, :]
        fy = here(1)
        vy = here(4) + here_low(4)
        vz = here(5) + here_low(5)
        return (vz + below(vz)) * (fy + below(fy)) - (vy + below(vy)) * (here(2) + here_low(2))

    def new_cells(i, row, emf_z, emf_y, emf_x, next_z, next_y, beyond_z, beyond_x):
        lift = lambda values, beyond: jnp.where(level == 7, beyond, pltpu.roll(values, 7, axis=0))
        new_x = ext[0, i + 1, row : row + 8, :] - SCALE * (
            (lift(emf_z, beyond_z) - emf_z) - (above(emf_y) - emf_y)
        )
        new_y = ext[1, i + 1, row : row + 8, :] - SCALE * (
            (above(emf_x) - emf_x) - (next_z - emf_z)
        )
        new_z = ext[2, i + 1, row : row + 8, :] - SCALE * (
            (next_y - emf_y) - (lift(emf_x, beyond_x) - emf_x)
        )
        return new_x, new_y, new_z

    def upper_rows(start, count, pack, offset):
        def step(n, carried):
            i = start + n
            emf_z, emf_y = carried
            next_z, next_y = side_edges(i + 1, 16)
            emf_x = cross_edge(i, 16)
            top_edges[0, i] = emf_z
            top_edges[1, i] = emf_x
            cells = new_cells(i, 16, emf_z, emf_y, emf_x, next_z, next_y, 0.0, 0.0)
            for part, values in enumerate(cells):
                updated[part, i, 8:16, :] = values
                pack[part, n + offset] = values
            return next_z, next_y

        lax.fori_loop(0, count, step, side_edges(start, 16))

    def spread_last(pack, strip):
        for part in range(3):
            for n in range(7):
                pack[part, n, 0:1, :] = updated[part, strip, 9 + n : 10 + n, :]

    quarter = strips // 4
    half = strips // 2
    upper_rows(quarter, half - 1, pack_a, 0)

    def one_upper(i):
        emf_z, emf_y = side_edges(i, 16)
        next_z, next_y = side_edges(i + 1, 16)
        emf_x = cross_edge(i, 16)
        top_edges[0, i] = emf_z
        top_edges[1, i] = emf_x
        cells = new_cells(i, 16, emf_z, emf_y, emf_x, next_z, next_y, 0.0, 0.0)
        for part, values in enumerate(cells):
            updated[part, i, 8:16, :] = values

    one_upper(quarter + half - 1)
    spread_last(pack_a, quarter + half - 1)
    near_copy_a.start()

    for copy in scalars:
        copy.wait()
    for copy in (up_f, up_v, down_f, down_v):
        copy.wait_recv()

    @pl.when(first)
    def _():
        shear_up_f.wait_recv()
        shear_up_v.wait_recv()
        shift = edge_shift[0]
        weight = edge_frac[0]
        for part in range(1, 6):
            rows = low_raw[part]
            mixed = (1.0 - weight) * rows + weight * pltpu.roll(rows, 1, axis=0)
            ext[part, 0, :, :] = pltpu.roll(mixed, shift, axis=0)

    @pl.when(jnp.logical_not(first))
    def _():
        for part in range(1, 6):
            ext[part, 0, 8:24, :] = low_raw[part, 8:24, :]

    @pl.when(last)
    def _():
        shear_down_f.wait_recv()
        shear_down_v.wait_recv()
        shift = edge_shift[1]
        weight = edge_frac[1]
        for part in range(6):
            rows = high_raw[part]
            mixed = (1.0 - weight) * rows + weight * pltpu.roll(rows, 31, axis=0)
            ext[part, strips + 1, 8:24, :] = pltpu.roll(mixed, lax.rem(32 - shift, 32), axis=0)[8:24]

    @pl.when(jnp.logical_not(last))
    def _():
        for part in range(6):
            ext[part, strips + 1, 8:24, :] = high_raw[part, 8:24, :]

    row_up.wait_recv()
    corner_up.start()
    corner_down.start()

    upper_rows(strips - quarter, quarter, pack_b, 0)
    upper_rows(0, quarter - 1, pack_b, quarter)
    one_upper(quarter - 1)
    spread_last(pack_b, quarter - 1)
    near_copy_b.start()

    for n, part in enumerate(row_parts):
        for i in range(strips):
            ext[part, i + 1, 7:8, :] = row_recv[n, i : i + 1, :]

    corner_up.wait_recv()
    corner_down.wait_recv()

    @pl.when(jnp.logical_not(first))
    def _():
        for n, part in enumerate((3, 4)):
            ext[part, 0, 7:8, :] = low_corner[n, 7:8, :]

    @pl.when(last)
    def _():
        shift = edge_shift[1]
        weight = edge_frac[1]
        for n, part in enumerate((0, 3, 4)):
            high_raw[part, 7:8, :] = high_corner[n, 0:1, :]
            rows = high_raw[part, 0:16, :]
            mixed = (1.0 - weight) * rows + weight * pltpu.roll(rows, 15, axis=0)
            ext[part, strips + 1, 7:8, :] = pltpu.roll(mixed, lax.rem(16 - shift, 16), axis=0)[7:8]

    @pl.when(jnp.logical_not(last))
    def _():
        for n, part in enumerate((0, 3, 4)):
            ext[part, strips + 1, 7:8, :] = high_corner[n, 0:1, :]

    def lower_rows(start, count, near, offset):
        def step(n, carried):
            i = start + n
            emf_z, emf_y = carried
            next_z, next_y = side_edges(i + 1, 8)
            emf_x = cross_edge(i, 8)
            bottom_edges[0, i] = emf_z
            bottom_edges[1, i] = emf_x
            cells = new_cells(
                i,
                8,
                emf_z,
                emf_y,
                emf_x,
                next_z,
                next_y,
                pltpu.roll(top_edges[0, i], 7, axis=0),
                pltpu.roll(top_edges[1, i], 7, axis=0),
            )
            for part, values in enumerate(cells):
                updated[part, i, 0:8, :] = values
                near[part, n + offset, 8:16, :] = values
            return next_z, next_y

        lax.fori_loop(0, count, step, side_edges(start, 8))

    lower_rows(0, quarter, near_b, quarter)
    lower_rows(quarter, half, near_a, 0)
    lower_rows(strips - quarter, quarter, near_b, 0)
    for n in range(2):
        for i in range(strips):
            edge_send[n, i : i + 1, :] = bottom_edges[n, i, 0:1, :]
    edges_down.start()

    edges_down.wait_recv()

    def blend_upper(i, _):
        updated[0, i, 15:16, :] = updated[0, i, 15:16, :] - SCALE * edge_recv[0, pl.ds(i, 1), :]
        updated[2, i, 15:16, :] = updated[2, i, 15:16, :] + SCALE * edge_recv[1, pl.ds(i, 1), :]
        shift = strip_shift[i]
        weight = strip_frac[i]
        for part in range(3):
            rows = updated[part, i]
            mixed = (1.0 - weight) * rows + weight * pltpu.roll(rows, 1, axis=0)
            result[part, i, 8:16, :] = pltpu.roll(mixed, shift, axis=0)[8:16]
        return 0

    lax.fori_loop(0, strips, blend_upper, 0)
    stores = [
        pltpu.make_async_copy(
            result.at[:, places, rows, :], out.at[:, places, rows, :], store_sem.at[n]
        )
        for n, (places, rows) in enumerate(
            (
                (slice(0, strips), slice(8, 16)),
                (slice(quarter, quarter + half), slice(0, 8)),
                (slice(strips - quarter, strips), slice(0, 8)),
                (slice(0, quarter), slice(0, 8)),
            )
        )
    ]
    stores[0].start()

    def blend_lower(near, start):
        for part in range(3):
            for n in range(7):
                near[part, 7, n + 1 : n + 2, :] = near[part, n, 0:1, :]

        def step(n, _):
            i = lax.rem(start + n, strips)
            near[0, n, 7:8, :] = near[0, n, 7:8, :] - SCALE * bottom_edges[0, i, 0:1, :]
            near[2, n, 7:8, :] = near[2, n, 7:8, :] + SCALE * bottom_edges[1, i, 0:1, :]
            shift = strip_shift[i]
            weight = strip_frac[i]
            for part in range(3):
                rows = near[part, n]
                mixed = (1.0 - weight) * rows + weight * pltpu.roll(rows, 1, axis=0)
                result[part, i, 0:8, :] = pltpu.roll(mixed, shift, axis=0)[8:16]
            return 0

        lax.fori_loop(0, half, step, 0)

    near_copy_a.wait_recv()
    blend_lower(near_a, quarter)
    stores[1].start()
    near_copy_b.wait_recv()
    blend_lower(near_b, strips - quarter)
    stores[2].start()
    stores[3].start()

    for copy in (up_f, up_v, down_f, down_v, row_up, corner_up, corner_down):
        copy.wait_send()
    for copy in (near_copy_a, near_copy_b, edges_down):
        copy.wait_send()

    @pl.when(last)
    def _():
        shear_up_f.wait_send()
        shear_up_v.wait_send()

    @pl.when(first)
    def _():
        shear_down_f.wait_send()
        shear_down_v.wait_send()

    for store in stores:
        store.wait()


def body(mesh_shape, field, velocity, strip_shift, strip_frac, edge_shift, edge_frac):
    parts, strips, azimuth, wide = field.shape
    half = strips // 2
    f32 = jnp.float32
    hbm = pl.BlockSpec(memory_space=pltpu.HBM)
    return pl.pallas_call(
        functools.partial(kernel, mesh_shape["blocks"], mesh_shape["phi"]),
        out_shape=jax.ShapeDtypeStruct(field.shape, f32),
        in_specs=[hbm] * 6,
        out_specs=hbm,
        scratch_shapes=[
            pltpu.VMEM((6, strips + 2, 8 + azimuth, wide), f32),
            pltpu.VMEM((6, 24, wide), f32),
            pltpu.VMEM((6, 32, wide), f32),
            pltpu.VMEM((2, 8, wide), f32),
            pltpu.VMEM((3, 8, wide), f32),
            pltpu.VMEM((5, strips, wide), f32),
            pltpu.VMEM((5, strips, wide), f32),
            pltpu.VMEM((2, strips, 8, wide), f32),
            pltpu.VMEM((2, strips, 8, wide), f32),
            pltpu.VMEM((2, strips, wide), f32),
            pltpu.VMEM((2, strips, wide), f32),
            pltpu.VMEM((3, strips, azimuth, wide), f32),
            pltpu.VMEM((3, 7, 8, wide), f32),
            pltpu.VMEM((3, 7, 8, wide), f32),
            pltpu.VMEM((3, half, 16, wide), f32),
            pltpu.VMEM((3, half, 16, wide), f32),
            pltpu.VMEM((3, strips, azimuth, wide), f32),
            pltpu.SMEM(strip_shift.shape, jnp.int32),
            pltpu.SMEM(strip_frac.shape, f32),
            pltpu.SMEM(edge_shift.shape, jnp.int32),
            pltpu.SMEM(edge_frac.shape, f32),
            pltpu.SemaphoreType.DMA((8,)),
            pltpu.SemaphoreType.DMA((4,)),
            pltpu.SemaphoreType.DMA((14,)),
            pltpu.SemaphoreType.DMA((14,)),
        ],
        compiler_params=pltpu.CompilerParams(
            collective_id=0, has_side_effects=True, vmem_limit_bytes=64 * 1024 * 1024 - 65536
        ),
    )(field, velocity, strip_shift, strip_frac, edge_shift, edge_frac)


def solution(mesh):
    placed = (
        P(None, "blocks", "phi", None),
        P(None, "blocks", "phi", None),
        P("blocks"),
        P("blocks"),
        P(),
        P(),
    )
    return jax.shard_map(
        functools.partial(body, dict(mesh.shape)),
        mesh=mesh,
        in_specs=placed,
        out_specs=P(None, "blocks", "phi", None),
        check_vma=False,
    )
```

```python
import functools

import jax
import jax.numpy as jnp
from jax import lax
from jax.experimental import pallas as pl
from jax.experimental.pallas import tpu as pltpu
from jax.sharding import PartitionSpec as P

COURANT = 0.4
SCALE = COURANT * 0.125
MESH = pl.DeviceIdType.MESH


def kernel(
    blocks,
    phis,
    field,
    velocity,
    shift_in,
    frac_in,
    edge_shift_in,
    edge_frac_in,
    out,
    ext,
    low_raw,
    high_raw,
    low_corner,
    high_corner,
    row_send,
    row_recv,
    top_edges,
    bottom_edges,
    edge_send,
    edge_recv,
    updated,
    pack_a,
    pack_b,
    near_a,
    near_b,
    strip_shift,
    strip_frac,
    edge_shift,
    edge_frac,
    load_sem,
    send_sem,
    recv_sem,
):
    b = lax.axis_index("blocks")
    p = lax.axis_index("phi")
    b_up = lax.rem(b + 1, blocks)
    b_down = lax.rem(b + blocks - 1, blocks)
    p_up = lax.rem(p + 1, phis)
    p_down = lax.rem(p + phis - 1, phis)
    first = b == 0
    last = b == blocks - 1
    strips = field.shape[1]
    wide = field.shape[3]

    loads = [
        pltpu.make_async_copy(
            source.at[:, :, rows, :],
            ext.at[part, 1 : strips + 1, pl.ds(8 + rows.start, 8), :],
            load_sem.at[n],
        )
        for n, (source, part, rows) in enumerate(
            (
                (field, slice(0, 3), slice(8, 16)),
                (velocity, slice(3, 6), slice(8, 16)),
                (field, slice(0, 3), slice(0, 8)),
                (velocity, slice(3, 6), slice(0, 8)),
            )
        )
    ]
    for load in loads[0:2]:
        load.start()
    scalars = [
        pltpu.make_async_copy(source, target, load_sem.at[4 + n])
        for n, (source, target) in enumerate(
            (
                (shift_in, strip_shift),
                (frac_in, strip_frac),
                (edge_shift_in, edge_shift),
                (edge_frac_in, edge_frac),
            )
        )
    ]
    for copy in scalars:
        copy.start()

    barrier = pltpu.get_barrier_semaphore()
    for device in ((b_up, p), (b_down, p), (b, p_up), (b, p_down)):
        pl.semaphore_signal(barrier, inc=1, device_id=device, device_id_type=MESH)

    @pl.when(first)
    def _():
        pl.semaphore_signal(barrier, inc=1, device_id=(b_down, p_down), device_id_type=MESH)

    @pl.when(last)
    def _():
        pl.semaphore_signal(barrier, inc=1, device_id=(b_up, p_up), device_id_type=MESH)

    pl.semaphore_wait(barrier, jnp.where(jnp.logical_or(first, last), 5, 4))

    def remote(n, source, target, device):
        return pltpu.make_async_remote_copy(
            src_ref=source,
            dst_ref=target,
            send_sem=send_sem.at[n],
            recv_sem=recv_sem.at[n],
            device_id=device,
            device_id_type=MESH,
        )

    end = strips - 1
    up_f = remote(0, field.at[1:3, end], low_raw.at[1:3, 8:24], (b_up, p))
    up_v = remote(1, velocity.at[:, end], low_raw.at[3:6, 8:24], (b_up, p))
    down_f = remote(2, field.at[:, 0], high_raw.at[0:3, 8:24], (b_down, p))
    down_v = remote(3, velocity.at[:, 0], high_raw.at[3:6, 8:24], (b_down, p))
    shear_up_f = remote(4, field.at[1:3, end, 8:16], low_raw.at[1:3, 0:8], (b_up, p_up))
    shear_up_v = remote(5, velocity.at[:, end, 8:16], low_raw.at[3:6, 0:8], (b_up, p_up))
    shear_down = remote(6, high_raw.at[:, 8:16], high_raw.at[:, 24:32], (b, p_down))
    row_up = remote(8, row_send, row_recv, (b, p_up))
    corner_up = remote(9, row_recv.at[1:3, strips - 8 : strips], low_corner, (b_up, p))
    corner_down = remote(10, row_recv.at[0:3, 0:8], high_corner, (b_down, p))
    edges_down = remote(7, edge_send, edge_recv, (b, p_down))
    near_copy_a, near_copy_b = (
        [
            remote(n + part, pack.at[part], near.at[part, 0:7, 0:8], (b, p_up))
            for part in range(3)
        ]
        for n, pack, near in ((11, pack_a, near_a), (14, pack_b, near_b))
    )

    for copy in (up_f, up_v, down_f, down_v):
        copy.start()

    @pl.when(last)
    def _():
        shear_up_f.start()
        shear_up_v.start()

    row_parts = (0, 3, 4, 5, 2)
    loads[0].wait()
    loads[1].wait()
    loads[2].start()
    loads[3].start()
    for n, part in enumerate(row_parts):
        for i in range(strips):
            row_send[n, i : i + 1, :] = ext[part, i + 1, 23:24, :]
    row_up.start()
    loads[2].wait()
    loads[3].wait()

    level = lax.broadcasted_iota(jnp.int32, (8, wide), 0)

    def below(values):
        return pltpu.roll(values, 1, axis=1)

    def above(values):
        return pltpu.roll(values, wide - 1, axis=1)

    def side_edges(i, row):
        here = lambda part: ext[part, i + 1, row : row + 8, :]
        inner = lambda part: ext[part, i, row : row + 8, :]
        here_low = lambda part: ext[part, i + 1, row - 1 : row + 7, :]
        inner_low = lambda part: ext[part, i, row - 1 : row + 7, :]
        fx = here(0)
        vx = here(3) + inner(3)
        vz = here(5) + inner(5)
        vx_all = vx + here_low(3) + inner_low(3)
        vy_all = here(4) + inner(4) + here_low(4) + inner_low(4)
        emf_z = vy_all * (fx + here_low(0)) - vx_all * (here(1) + inner(1))
        emf_y = (vx + below(vx)) * (here(2) + inner(2)) - (vz + below(vz)) * (fx + below(fx))
        return emf_z, emf_y

    def cross_edge(i, row):
        here = lambda part: ext[part, i + 1, row : row + 8, :]
        here_low = lambda part: ext[part, i + 1, row - 1 : row + 7, :]
        fy = here(1)
        vy = here(4) + here_low(4)
        vz = here(5) + here_low(5)
        return (vz + below(vz)) * (fy + below(fy)) - (vy + below(vy)) * (here(2) + here_low(2))

    def new_cells(i, row, emf_z, emf_y, emf_x, next_z, next_y, beyond_z, beyond_x):
        lift = lambda values, beyond: jnp.where(level == 7, beyond, pltpu.roll(values, 7, axis=0))
        new_x = ext[0, i + 1, row : row + 8, :] - SCALE * (
            (lift(emf_z, beyond_z) - emf_z) - (above(emf_y) - emf_y)
        )
        new_y = ext[1, i + 1, row : row + 8, :] - SCALE * (
            (above(emf_x) - emf_x) - (next_z - emf_z)
        )
        new_z = ext[2, i + 1, row : row + 8, :] - SCALE * (
            (next_y - emf_y) - (lift(emf_x, beyond_x) - emf_x)
        )
        return new_x, new_y, new_z

    def upper_rows(start, count, pack, offset):
        def step(n, carried):
            i = start + n
            emf_z, emf_y = carried
            next_z, next_y = side_edges(i + 1, 16)
            emf_x = cross_edge(i, 16)
            top_edges[0, i] = emf_z
            top_edges[1, i] = emf_x
            cells = new_cells(i, 16, emf_z, emf_y, emf_x, next_z, next_y, 0.0, 0.0)
            for part, values in enumerate(cells):
                updated[part, i, 8:16, :] = values
                pack[part, n + offset] = values
            return next_z, next_y

        lax.fori_loop(0, count, step, side_edges(start, 16))

    def spread_last(pack, strip):
        for part in range(3):
            for n in range(7):
                pack[part, n, 0:1, :] = updated[part, strip, 9 + n : 10 + n, :]

    quarter = strips // 4
    half = strips // 2
    upper_rows(quarter, half - 1, pack_a, 0)

    def one_upper(i):
        emf_z, emf_y = side_edges(i, 16)
        next_z, next_y = side_edges(i + 1, 16)
        emf_x = cross_edge(i, 16)
        top_edges[0, i] = emf_z
        top_edges[1, i] = emf_x
        cells = new_cells(i, 16, emf_z, emf_y, emf_x, next_z, next_y, 0.0, 0.0)
        for part, values in enumerate(cells):
            updated[part, i, 8:16, :] = values

    one_upper(quarter + half - 1)
    spread_last(pack_a, quarter + half - 1)
    for copy in near_copy_a:
        copy.start()

    for copy in scalars:
        copy.wait()
    for copy in (up_f, up_v, down_f, down_v):
        copy.wait_recv()

    @pl.when(first)
    def _():
        shear_up_f.wait_recv()
        shear_up_v.wait_recv()
        shift = edge_shift[0]
        weight = edge_frac[0]
        for part in range(1, 6):
            rows = low_raw[part]
            mixed = (1.0 - weight) * rows + weight * pltpu.roll(rows, 1, axis=0)
            ext[part, 0, :, :] = pltpu.roll(mixed, shift, axis=0)

    @pl.when(jnp.logical_not(first))
    def _():
        for part in range(1, 6):
            ext[part, 0, 8:24, :] = low_raw[part, 8:24, :]

    @pl.when(last)
    def _():
        shear_down.start()
        shear_down.wait_recv()
        shift = edge_shift[1]
        weight = edge_frac[1]
        for part in range(6):
            rows = high_raw[part]
            mixed = (1.0 - weight) * rows + weight * pltpu.roll(rows, 31, axis=0)
            ext[part, strips + 1, 8:24, :] = pltpu.roll(mixed, lax.rem(32 - shift, 32), axis=0)[8:24]

    @pl.when(jnp.logical_not(last))
    def _():
        for part in range(6):
            ext[part, strips + 1, 8:24, :] = high_raw[part, 8:24, :]

    row_up.wait_recv()
    corner_up.start()
    corner_down.start()

    upper_rows(strips - quarter, quarter, pack_b, 0)
    upper_rows(0, quarter - 1, pack_b, quarter)
    one_upper(quarter - 1)
    spread_last(pack_b, quarter - 1)
    for copy in near_copy_b:
        copy.start()

    for n, part in enumerate(row_parts):
        for i in range(strips):
            ext[part, i + 1, 7:8, :] = row_recv[n, i : i + 1, :]

    corner_up.wait_recv()
    corner_down.wait_recv()

    @pl.when(jnp.logical_not(first))
    def _():
        for n, part in enumerate((3, 4)):
            ext[part, 0, 7:8, :] = low_corner[n, 7:8, :]

    @pl.when(last)
    def _():
        shift = edge_shift[1]
        weight = edge_frac[1]
        for n, part in enumerate((0, 3, 4)):
            high_raw[part, 7:8, :] = high_corner[n, 0:1, :]
            rows = high_raw[part, 0:16, :]
            mixed = (1.0 - weight) * rows + weight * pltpu.roll(rows, 15, axis=0)
            ext[part, strips + 1, 7:8, :] = pltpu.roll(mixed, lax.rem(16 - shift, 16), axis=0)[7:8]

    @pl.when(jnp.logical_not(last))
    def _():
        for n, part in enumerate((0, 3, 4)):
            ext[part, strips + 1, 7:8, :] = high_corner[n, 0:1, :]

    def lower_rows(start, count, near, offset):
        def step(n, carried):
            i = start + n
            emf_z, emf_y = carried
            next_z, next_y = side_edges(i + 1, 8)
            emf_x = cross_edge(i, 8)
            bottom_edges[0, i] = emf_z
            bottom_edges[1, i] = emf_x
            cells = new_cells(
                i,
                8,
                emf_z,
                emf_y,
                emf_x,
                next_z,
                next_y,
                pltpu.roll(top_edges[0, i], 7, axis=0),
                pltpu.roll(top_edges[1, i], 7, axis=0),
            )
            for part, values in enumerate(cells):
                updated[part, i, 0:8, :] = values
                near[part, n + offset, 8:16, :] = values
            return next_z, next_y

        lax.fori_loop(0, count, step, side_edges(start, 8))

    lower_rows(0, quarter, near_b, quarter)
    lower_rows(quarter, half, near_a, 0)
    lower_rows(strips - quarter, quarter, near_b, 0)
    for n in range(2):
        for i in range(strips):
            edge_send[n, i : i + 1, :] = bottom_edges[n, i, 0:1, :]
    edges_down.start()

    edges_down.wait_recv()

    def blend_upper(i, _):
        updated[0, i, 15:16, :] = updated[0, i, 15:16, :] - SCALE * edge_recv[0, pl.ds(i, 1), :]
        updated[2, i, 15:16, :] = updated[2, i, 15:16, :] + SCALE * edge_recv[1, pl.ds(i, 1), :]
        shift = strip_shift[i]
        weight = strip_frac[i]
        for part in range(3):
            rows = updated[part, i]
            mixed = (1.0 - weight) * rows + weight * pltpu.roll(rows, 1, axis=0)
            out[part, i, 8:16, :] = pltpu.roll(mixed, shift, axis=0)[8:16]
        return 0

    lax.fori_loop(0, strips, blend_upper, 0)
    def blend_lower(near, start, part):
        for n in range(7):
            near[part, 7, n + 1 : n + 2, :] = near[part, n, 0:1, :]

        def step(n, _):
            i = lax.rem(start + n, strips)
            rows = near[part, n]
            if part == 0:
                rows = rows - jnp.where(lowest, SCALE * bottom_edges[0, i, 0:1, :], 0.0)
            if part == 2:
                rows = rows + jnp.where(lowest, SCALE * bottom_edges[1, i, 0:1, :], 0.0)
            weight = strip_frac[i]
            mixed = (1.0 - weight) * rows + weight * pltpu.roll(rows, 1, axis=0)
            out[part, i, 0:8, :] = pltpu.roll(mixed, strip_shift[i], axis=0)[8:16]
            return 0

        lax.fori_loop(0, half, step, 0)

    lowest = lax.broadcasted_iota(jnp.int32, (16, wide), 0) == 7
    for part in range(3):
        near_copy_a[part].wait_recv()
        blend_lower(near_a, quarter, part)
    for part in range(3):
        near_copy_b[part].wait_recv()
        blend_lower(near_b, strips - quarter, part)

    for copy in (up_f, up_v, down_f, down_v, row_up, corner_up, corner_down):
        copy.wait_send()
    for copy in (*near_copy_a, *near_copy_b, edges_down):
        copy.wait_send()

    @pl.when(last)
    def _():
        shear_up_f.wait_send()
        shear_up_v.wait_send()
        shear_down.wait_send()


def body(mesh_shape, field, velocity, strip_shift, strip_frac, edge_shift, edge_frac):
    parts, strips, azimuth, wide = field.shape
    half = strips // 2
    f32 = jnp.float32
    hbm = pl.BlockSpec(memory_space=pltpu.HBM)
    return pl.pallas_call(
        functools.partial(kernel, mesh_shape["blocks"], mesh_shape["phi"]),
        out_shape=pltpu.VMEM(field.shape, f32),
        in_specs=[hbm] * 6,
        out_specs=pl.BlockSpec(memory_space=pltpu.VMEM),
        scratch_shapes=[
            pltpu.VMEM((6, strips + 2, 8 + azimuth, wide), f32),
            pltpu.VMEM((6, 24, wide), f32),
            pltpu.VMEM((6, 32, wide), f32),
            pltpu.VMEM((2, 8, wide), f32),
            pltpu.VMEM((3, 8, wide), f32),
            pltpu.VMEM((5, strips, wide), f32),
            pltpu.VMEM((5, strips, wide), f32),
            pltpu.VMEM((2, strips, 8, wide), f32),
            pltpu.VMEM((2, strips, 8, wide), f32),
            pltpu.VMEM((2, strips, wide), f32),
            pltpu.VMEM((2, strips, wide), f32),
            pltpu.VMEM((3, strips, azimuth, wide), f32),
            pltpu.VMEM((3, 7, 8, wide), f32),
            pltpu.VMEM((3, 7, 8, wide), f32),
            pltpu.VMEM((3, half, 16, wide), f32),
            pltpu.VMEM((3, half, 16, wide), f32),
            pltpu.SMEM(strip_shift.shape, jnp.int32),
            pltpu.SMEM(strip_frac.shape, f32),
            pltpu.SMEM(edge_shift.shape, jnp.int32),
            pltpu.SMEM(edge_frac.shape, f32),
            pltpu.SemaphoreType.DMA((8,)),
            pltpu.SemaphoreType.DMA((17,)),
            pltpu.SemaphoreType.DMA((17,)),
        ],
        compiler_params=pltpu.CompilerParams(
            collective_id=0, has_side_effects=True, vmem_limit_bytes=62 * 1024 * 1024
        ),
    )(field, velocity, strip_shift, strip_frac, edge_shift, edge_frac)


def solution(mesh):
    placed = (
        P(None, "blocks", "phi", None),
        P(None, "blocks", "phi", None),
        P("blocks"),
        P("blocks"),
        P(),
        P(),
    )
    return jax.shard_map(
        functools.partial(body, dict(mesh.shape)),
        mesh=mesh,
        in_specs=placed,
        out_specs=P(None, "blocks", "phi", None),
        check_vma=False,
    )
```

```python
import functools

import jax
import jax.numpy as jnp
from jax import lax
from jax.experimental import pallas as pl
from jax.experimental.pallas import tpu as pltpu
from jax.sharding import PartitionSpec as P

COURANT = 0.4
SCALE = COURANT * 0.125
MESH = pl.DeviceIdType.MESH


def kernel(
    blocks,
    phis,
    field,
    velocity,
    shift_in,
    frac_in,
    edge_shift_in,
    edge_frac_in,
    out,
    ext,
    low_raw,
    high_raw,
    low_corner,
    high_corner,
    row_send,
    row_recv,
    top_edges,
    bottom_edges,
    edge_send,
    edge_recv,
    updated,
    pack_a,
    pack_b,
    near_a,
    near_b,
    strip_shift,
    strip_frac,
    edge_shift,
    edge_frac,
    load_sem,
    send_sem,
    recv_sem,
):
    b = lax.axis_index("blocks")
    p = lax.axis_index("phi")
    b_up = lax.rem(b + 1, blocks)
    b_down = lax.rem(b + blocks - 1, blocks)
    p_up = lax.rem(p + 1, phis)
    p_down = lax.rem(p + phis - 1, phis)
    first = b == 0
    last = b == blocks - 1
    strips = field.shape[1]
    wide = field.shape[3]

    loads = [
        pltpu.make_async_copy(
            source.at[:, :, rows, :],
            ext.at[part, 1 : strips + 1, pl.ds(8 + rows.start, 8), :],
            load_sem.at[n],
        )
        for n, (source, part, rows) in enumerate(
            (
                (field, slice(0, 3), slice(8, 16)),
                (velocity, slice(3, 6), slice(8, 16)),
                (field, slice(0, 3), slice(0, 8)),
                (velocity, slice(3, 6), slice(0, 8)),
            )
        )
    ]
    for load in loads[0:2]:
        load.start()
    scalars = [
        pltpu.make_async_copy(source, target, load_sem.at[4 + n])
        for n, (source, target) in enumerate(
            (
                (shift_in, strip_shift),
                (frac_in, strip_frac),
                (edge_shift_in, edge_shift),
                (edge_frac_in, edge_frac),
            )
        )
    ]
    for copy in scalars:
        copy.start()

    barrier = pltpu.get_barrier_semaphore()
    for device in ((b_up, p), (b_down, p), (b, p_up), (b, p_down)):
        pl.semaphore_signal(barrier, inc=1, device_id=device, device_id_type=MESH)

    @pl.when(first)
    def _():
        pl.semaphore_signal(barrier, inc=1, device_id=(b_down, p_down), device_id_type=MESH)

    @pl.when(last)
    def _():
        pl.semaphore_signal(barrier, inc=1, device_id=(b_up, p_up), device_id_type=MESH)

    pl.semaphore_wait(barrier, jnp.where(jnp.logical_or(first, last), 5, 4))

    def remote(n, source, target, device):
        return pltpu.make_async_remote_copy(
            src_ref=source,
            dst_ref=target,
            send_sem=send_sem.at[n],
            recv_sem=recv_sem.at[n],
            device_id=device,
            device_id_type=MESH,
        )

    end = strips - 1
    up_f = remote(0, field.at[1:3, end], low_raw.at[1:3, 8:24], (b_up, p))
    up_v = remote(1, velocity.at[:, end], low_raw.at[3:6, 8:24], (b_up, p))
    down_f = remote(2, field.at[:, 0], high_raw.at[0:3, 8:24], (b_down, p))
    down_v = remote(3, velocity.at[:, 0], high_raw.at[3:6, 8:24], (b_down, p))
    shear_up_f = remote(4, field.at[1:3, end, 8:16], low_raw.at[1:3, 0:8], (b_up, p_up))
    shear_up_v = remote(5, velocity.at[:, end, 8:16], low_raw.at[3:6, 0:8], (b_up, p_up))
    shear_down_f = remote(6, field.at[:, 0, 0:8], high_raw.at[0:3, 24:32], (b_down, p_down))
    shear_down_v = remote(17, velocity.at[:, 0, 0:8], high_raw.at[3:6, 24:32], (b_down, p_down))
    row_up = remote(8, row_send, row_recv, (b, p_up))
    corner_up = remote(9, row_recv.at[1:3, strips - 8 : strips], low_corner, (b_up, p))
    corner_down = remote(10, row_recv.at[0:3, 0:8], high_corner, (b_down, p))
    edges_down = remote(7, edge_send, edge_recv, (b, p_down))
    near_copy_a = [
        remote(11 + part, pack_a.at[part], near_a.at[part, 0:7, 0:8], (b, p_up))
        for part in range(3)
    ]
    near_copy_b = [
        remote(14 + n, pack_b.at[:, tiles], near_b.at[:, tiles, 0:8], (b, p_up))
        for n, tiles in enumerate((slice(0, 3), slice(5, 7), slice(3, 5)))
    ]

    @pl.when(last)
    def _():
        shear_up_f.start()
        shear_up_v.start()

    @pl.when(first)
    def _():
        shear_down_f.start()
        shear_down_v.start()

    for copy in (up_f, up_v, down_f, down_v):
        copy.start()

    row_parts = (0, 3, 4, 5, 2)
    loads[0].wait()
    loads[1].wait()
    loads[2].start()
    loads[3].start()
    for n, part in enumerate(row_parts):
        for i in range(strips):
            row_send[n, i : i + 1, :] = ext[part, i + 1, 23:24, :]
    row_up.start()
    loads[2].wait()
    loads[3].wait()

    level = lax.broadcasted_iota(jnp.int32, (8, wide), 0)

    def below(values):
        return pltpu.roll(values, 1, axis=1)

    def above(values):
        return pltpu.roll(values, wide - 1, axis=1)

    def side_edges(i, row):
        here = lambda part: ext[part, i + 1, row : row + 8, :]
        inner = lambda part: ext[part, i, row : row + 8, :]
        here_low = lambda part: ext[part, i + 1, row - 1 : row + 7, :]
        inner_low = lambda part: ext[part, i, row - 1 : row + 7, :]
        fx = here(0)
        vx = here(3) + inner(3)
        vz = here(5) + inner(5)
        vx_all = vx + here_low(3) + inner_low(3)
        vy_all = here(4) + inner(4) + here_low(4) + inner_low(4)
        emf_z = vy_all * (fx + here_low(0)) - vx_all * (here(1) + inner(1))
        emf_y = (vx + below(vx)) * (here(2) + inner(2)) - (vz + below(vz)) * (fx + below(fx))
        return emf_z, emf_y

    def cross_edge(i, row):
        here = lambda part: ext[part, i + 1, row : row + 8, :]
        here_low = lambda part: ext[part, i + 1, row - 1 : row + 7, :]
        fy = here(1)
        vy = here(4) + here_low(4)
        vz = here(5) + here_low(5)
        return (vz + below(vz)) * (fy + below(fy)) - (vy + below(vy)) * (here(2) + here_low(2))

    def new_cells(i, row, emf_z, emf_y, emf_x, next_z, next_y, beyond_z, beyond_x):
        lift = lambda values, beyond: jnp.where(level == 7, beyond, pltpu.roll(values, 7, axis=0))
        new_x = ext[0, i + 1, row : row + 8, :] - SCALE * (
            (lift(emf_z, beyond_z) - emf_z) - (above(emf_y) - emf_y)
        )
        new_y = ext[1, i + 1, row : row + 8, :] - SCALE * (
            (above(emf_x) - emf_x) - (next_z - emf_z)
        )
        new_z = ext[2, i + 1, row : row + 8, :] - SCALE * (
            (next_y - emf_y) - (lift(emf_x, beyond_x) - emf_x)
        )
        return new_x, new_y, new_z

    def upper_rows(start, count, pack, offset):
        def step(n, carried):
            i = start + n
            emf_z, emf_y = carried
            next_z, next_y = side_edges(i + 1, 16)
            emf_x = cross_edge(i, 16)
            top_edges[0, i] = emf_z
            top_edges[1, i] = emf_x
            cells = new_cells(i, 16, emf_z, emf_y, emf_x, next_z, next_y, 0.0, 0.0)
            for part, values in enumerate(cells):
                updated[part, i, 8:16, :] = values
                pack[part, n + offset] = values
            return next_z, next_y

        lax.fori_loop(0, count, step, side_edges(start, 16))

    def spread_last(pack, strip, tiles):
        for part in range(3):
            for n in tiles:
                pack[part, n, 0:1, :] = updated[part, strip, 9 + n : 10 + n, :]

    quarter = strips // 4
    half = strips // 2
    upper_rows(quarter, half - 1, pack_a, 0)

    def one_upper(i):
        emf_z, emf_y = side_edges(i, 16)
        next_z, next_y = side_edges(i + 1, 16)
        emf_x = cross_edge(i, 16)
        top_edges[0, i] = emf_z
        top_edges[1, i] = emf_x
        cells = new_cells(i, 16, emf_z, emf_y, emf_x, next_z, next_y, 0.0, 0.0)
        for part, values in enumerate(cells):
            updated[part, i, 8:16, :] = values

    one_upper(quarter + half - 1)
    spread_last(pack_a, quarter + half - 1, range(7))
    for copy in near_copy_a:
        copy.start()

    upper_rows(strips - quarter, quarter - 1, pack_b, 0)
    upper_rows(1, quarter - 2, pack_b, quarter + 1)
    one_upper(quarter - 1)
    spread_last(pack_b, quarter - 1, (0, 1, 2, 5, 6))
    near_copy_b[0].start()
    near_copy_b[1].start()

    for copy in scalars:
        copy.wait()
    for copy in (up_f, up_v, down_f, down_v):
        copy.wait_recv()

    @pl.when(first)
    def _():
        shear_up_f.wait_recv()
        shear_up_v.wait_recv()
        shift = edge_shift[0]
        weight = edge_frac[0]
        for part in range(1, 6):
            rows = low_raw[part]
            mixed = (1.0 - weight) * rows + weight * pltpu.roll(rows, 1, axis=0)
            ext[part, 0, :, :] = pltpu.roll(mixed, shift, axis=0)

    @pl.when(jnp.logical_not(first))
    def _():
        for part in range(1, 6):
            ext[part, 0, 8:24, :] = low_raw[part, 8:24, :]

    @pl.when(last)
    def _():
        shear_down_f.wait_recv()
        shear_down_v.wait_recv()
        shift = edge_shift[1]
        weight = edge_frac[1]
        for part in range(6):
            rows = high_raw[part]
            mixed = (1.0 - weight) * rows + weight * pltpu.roll(rows, 31, axis=0)
            ext[part, strips + 1, 8:24, :] = pltpu.roll(mixed, lax.rem(32 - shift, 32), axis=0)[8:24]

    @pl.when(jnp.logical_not(last))
    def _():
        for part in range(6):
            ext[part, strips + 1, 8:24, :] = high_raw[part, 8:24, :]

    row_up.wait_recv()
    corner_up.start()
    corner_down.start()

    upper_rows(strips - 1, 1, pack_b, quarter - 1)
    upper_rows(0, 1, pack_b, quarter)
    spread_last(pack_b, quarter - 1, (3, 4))
    near_copy_b[2].start()

    for n, part in enumerate(row_parts):
        for i in range(strips):
            ext[part, i + 1, 7:8, :] = row_recv[n, i : i + 1, :]

    corner_up.wait_recv()
    corner_down.wait_recv()

    @pl.when(jnp.logical_not(first))
    def _():
        for n, part in enumerate((3, 4)):
            ext[part, 0, 7:8, :] = low_corner[n, 7:8, :]

    @pl.when(last)
    def _():
        shift = edge_shift[1]
        weight = edge_frac[1]
        for n, part in enumerate((0, 3, 4)):
            high_raw[part, 7:8, :] = high_corner[n, 0:1, :]
            rows = high_raw[part, 0:16, :]
            mixed = (1.0 - weight) * rows + weight * pltpu.roll(rows, 15, axis=0)
            ext[part, strips + 1, 7:8, :] = pltpu.roll(mixed, lax.rem(16 - shift, 16), axis=0)[7:8]

    @pl.when(jnp.logical_not(last))
    def _():
        for n, part in enumerate((0, 3, 4)):
            ext[part, strips + 1, 7:8, :] = high_corner[n, 0:1, :]

    def lower_rows(start, count, near, offset):
        def step(n, carried):
            i = start + n
            emf_z, emf_y = carried
            next_z, next_y = side_edges(i + 1, 8)
            emf_x = cross_edge(i, 8)
            bottom_edges[0, i] = emf_z
            bottom_edges[1, i] = emf_x
            cells = new_cells(
                i,
                8,
                emf_z,
                emf_y,
                emf_x,
                next_z,
                next_y,
                pltpu.roll(top_edges[0, i], 7, axis=0),
                pltpu.roll(top_edges[1, i], 7, axis=0),
            )
            for part, values in enumerate(cells):
                updated[part, i, 0:8, :] = values
                near[part, n + offset, 8:16, :] = values
            return next_z, next_y

        lax.fori_loop(0, count, step, side_edges(start, 8))

    lower_rows(0, quarter, near_b, quarter)
    lower_rows(quarter, half, near_a, 0)
    lower_rows(strips - quarter, quarter, near_b, 0)
    for n in range(2):
        for i in range(strips):
            edge_send[n, i : i + 1, :] = bottom_edges[n, i, 0:1, :]
    edges_down.start()

    edges_down.wait_recv()

    def blend_upper(i, _):
        updated[0, i, 15:16, :] = updated[0, i, 15:16, :] - SCALE * edge_recv[0, pl.ds(i, 1), :]
        updated[2, i, 15:16, :] = updated[2, i, 15:16, :] + SCALE * edge_recv[1, pl.ds(i, 1), :]
        shift = strip_shift[i]
        weight = strip_frac[i]
        for part in range(3):
            rows = updated[part, i]
            mixed = (1.0 - weight) * rows + weight * pltpu.roll(rows, 1, axis=0)
            out[part, i, 8:16, :] = pltpu.roll(mixed, shift, axis=0)[8:16]
        return 0

    lax.fori_loop(0, strips, blend_upper, 0)
    def blend_lower(near, start, part):
        for n in range(7):
            near[part, 7, n + 1 : n + 2, :] = near[part, n, 0:1, :]

        def step(n, _):
            i = lax.rem(start + n, strips)
            rows = near[part, n]
            if part == 0:
                rows = rows - jnp.where(lowest, SCALE * bottom_edges[0, i, 0:1, :], 0.0)
            if part == 2:
                rows = rows + jnp.where(lowest, SCALE * bottom_edges[1, i, 0:1, :], 0.0)
            weight = strip_frac[i]
            mixed = (1.0 - weight) * rows + weight * pltpu.roll(rows, 1, axis=0)
            out[part, i, 0:8, :] = pltpu.roll(mixed, strip_shift[i], axis=0)[8:16]
            return 0

        lax.fori_loop(0, half, step, 0)

    lowest = lax.broadcasted_iota(jnp.int32, (16, wide), 0) == 7
    for part in range(3):
        near_copy_a[part].wait_recv()
        blend_lower(near_a, quarter, part)
    for copy in near_copy_b:
        copy.wait_recv()
    for part in range(3):
        blend_lower(near_b, strips - quarter, part)

    for copy in (up_f, up_v, down_f, down_v, row_up, corner_up, corner_down):
        copy.wait_send()
    for copy in (*near_copy_a, *near_copy_b, edges_down):
        copy.wait_send()

    @pl.when(last)
    def _():
        shear_up_f.wait_send()
        shear_up_v.wait_send()

    @pl.when(first)
    def _():
        shear_down_f.wait_send()
        shear_down_v.wait_send()


def body(mesh_shape, field, velocity, strip_shift, strip_frac, edge_shift, edge_frac):
    parts, strips, azimuth, wide = field.shape
    half = strips // 2
    f32 = jnp.float32
    hbm = pl.BlockSpec(memory_space=pltpu.HBM)
    return pl.pallas_call(
        functools.partial(kernel, mesh_shape["blocks"], mesh_shape["phi"]),
        out_shape=pltpu.VMEM(field.shape, f32),
        in_specs=[hbm] * 6,
        out_specs=pl.BlockSpec(memory_space=pltpu.VMEM),
        scratch_shapes=[
            pltpu.VMEM((6, strips + 2, 8 + azimuth, wide), f32),
            pltpu.VMEM((6, 24, wide), f32),
            pltpu.VMEM((6, 32, wide), f32),
            pltpu.VMEM((2, 8, wide), f32),
            pltpu.VMEM((3, 8, wide), f32),
            pltpu.VMEM((5, strips, wide), f32),
            pltpu.VMEM((5, strips, wide), f32),
            pltpu.VMEM((2, strips, 8, wide), f32),
            pltpu.VMEM((2, strips, 8, wide), f32),
            pltpu.VMEM((2, strips, wide), f32),
            pltpu.VMEM((2, strips, wide), f32),
            pltpu.VMEM((3, strips, azimuth, wide), f32),
            pltpu.VMEM((3, 7, 8, wide), f32),
            pltpu.VMEM((3, 7, 8, wide), f32),
            pltpu.VMEM((3, half, 16, wide), f32),
            pltpu.VMEM((3, half, 16, wide), f32),
            pltpu.SMEM(strip_shift.shape, jnp.int32),
            pltpu.SMEM(strip_frac.shape, f32),
            pltpu.SMEM(edge_shift.shape, jnp.int32),
            pltpu.SMEM(edge_frac.shape, f32),
            pltpu.SemaphoreType.DMA((8,)),
            pltpu.SemaphoreType.DMA((18,)),
            pltpu.SemaphoreType.DMA((18,)),
        ],
        compiler_params=pltpu.CompilerParams(
            collective_id=0, has_side_effects=True, vmem_limit_bytes=62 * 1024 * 1024
        ),
    )(field, velocity, strip_shift, strip_frac, edge_shift, edge_frac)


def solution(mesh):
    placed = (
        P(None, "blocks", "phi", None),
        P(None, "blocks", "phi", None),
        P("blocks"),
        P("blocks"),
        P(),
        P(),
    )
    return jax.shard_map(
        functools.partial(body, dict(mesh.shape)),
        mesh=mesh,
        in_specs=placed,
        out_specs=P(None, "blocks", "phi", None),
        check_vma=False,
    )
```
